1024 devices in a mesh: group: 64 (over x, z), row: 16 (over y, core).
Axes of the slice: x: 4, y: 8, z: 16, core: 2. Of those that a mesh axis runs over, the one named last changes fastest.
Arguments:
- pooled_grad: bfloat16 [4096, 64, 128], P(('row', 'group')), may hold values from -0.59765625 to 0.59765625
- bag_ids: int32 [64, 40, 4096], P('group'), may hold values from 0 to 32767
- bag_len: int32 [64, 4096], P('group'), may hold values from 1 to 40
- table_rows: float32 [64, 32768, 128], P('group', 'row'), may hold values from -3 to 3
- row_state: float32 [64, 32768], P('group', 'row'), may hold values from 0.05 to 2
Outputs:
- new_rows: float32 [64, 32768, 128], P('group', 'row')
- new_state: float32 [64, 32768], P('group', 'row')
The draws below stay inside these ranges and needn't reach their ends.
All inputs are finite; a program needn't handle non-finite values.
Results may differ from the reference program's by a relative error of at most 0.0003.
Values may be sent and summed in bfloat16 or wider, within the bound.
A program may use at most 32 MiB of HBM per device.

```python
import math
import jax
import jax.numpy as jnp
from jax import lax

E = 128
BAG = 40
BATCH = 4096
TABLES = 64
ROWS = 32768


def touch_ends(result, rng, least, largest):
    place = [jax.random.randint(jax.random.fold_in(rng, axis), (), 0, length) for axis, length in enumerate(result.shape)]
    longest = result.shape.index(max(result.shape))
    neighbour = place[:longest] + [(place[longest] + 1) % result.shape[longest]] + place[longest + 1:]
    return result.at[tuple(place)].set(least).at[tuple(neighbour)].set(largest)


def block_levels(stream_key, dims, pieces, low, high):
    def one(dim, blocks):
        steps = jax.random.uniform(jax.random.fold_in(jax.random.fold_in(stream_key, 6), dim), (blocks,), jnp.float32, low / len(pieces), high / len(pieces))
        return jnp.repeat(jnp.exp(steps), dims[dim] // blocks).reshape((-1,) + (1,) * (len(dims) - dim - 1))

    gain = one(*pieces[0])
    for cut in pieces[1:]:
        gain = gain * one(*cut)
    return gain


def gaussian(rng, extent, deviation, most, cuts=(), dtype=jnp.bfloat16):
    result = deviation * jax.random.normal(rng, extent, jnp.float32)
    if cuts:
        result = result * block_levels(rng, extent, cuts, -0.22, 0.18)
    return jnp.clip(result, -most, most).astype(dtype)


def setup_inputs(seed: int = 0) -> dict:
    splits = jax.random.split(jax.random.key(seed), 6)
    return {
        "pooled_grad": gaussian(splits[0], (BATCH, TABLES, E), 0.1, 0.59765625, ((0, 1024),)),
        "bag_ids": touch_ends(jax.random.randint(splits[1], (TABLES, BAG, BATCH), 0, ROWS), jax.random.fold_in(splits[1], 1), 0, ROWS - 1).astype(jnp.int32),
        "bag_len": touch_ends(jax.random.randint(splits[2], (TABLES, BATCH), 1, BAG + 1), jax.random.fold_in(splits[2], 1), 1, BAG).astype(jnp.int32),
        "table_rows": gaussian(splits[3], (TABLES, ROWS, E), 0.5, 3.0, ((0, 64), (1, 16)), jnp.float32),
        "row_state": jnp.clip(jnp.exp(math.log(2.0) - 3.6888794 * jax.random.uniform(splits[4], (TABLES, ROWS), jnp.float32) ** block_levels(splits[4], (TABLES, ROWS), ((0, 64), (1, 16)), -0.2, 0.2)), 0.05, 2.0),
    }


def reference(pooled_grad, bag_ids, bag_len, table_rows, row_state):
    slots = jnp.arange(BAG).astype(jnp.int32)

    def one_table(table):
        ids_here = bag_ids[table]
        live = slots[:, None] < bag_len[table][None, :]
        grads_here = pooled_grad[:, table, :].astype(jnp.float32)
        values = jnp.where(live[:, :, None], grads_here[None, :, :], jnp.float32(0.0))
        return jnp.zeros((ROWS, E), jnp.float32).at[ids_here.reshape(-1)].add(values.reshape(-1, E))
    row_grad = lax.map(one_table, jnp.arange(TABLES).astype(jnp.int32))
    new_state = row_state + lax.optimization_barrier(jnp.mean(row_grad * row_grad, axis=2))
    new_rows = table_rows - 0.5 * row_grad / (jnp.sqrt(new_state)[:, :, None] + 1e-08)
    return (new_rows, new_state)
```

```python
import functools

import jax
import jax.numpy as jnp
from jax import lax
from jax.experimental import pallas as pl
from jax.experimental.pallas import tpu as pltpu
from jax.sharding import PartitionSpec as P

E = 128
SLOTS = 40
SAMPLES = 4096
GROUPS = 64
SHARDS = 16
WIDTH = 4
DEPTH = 16
RINGS = 8
EARLY = 6
VMEM = 60 * 2**20
TOUCHED = 2048
BLOCKS = 4
BLOCK = TOUCHED // BLOCKS
PARTS = 4
PART = TOUCHED // PARTS
FIELDS = 8
WORDS = TOUCHED // FIELDS
KEPT = 15
CHUNK = SAMPLES // SHARDS
MESH = pl.DeviceIdType.MESH


def prepare(ids, lens, keys, base):
    slot = lax.broadcasted_iota(jnp.int32, (8, 128), 0)

    def block(t, carry):
        lanes = pl.ds(pl.multiple_of(t * 128, 128), 128)
        used = lens[:, lanes]
        for q in range(SLOTS // 8):
            row = ids[pl.ds(8 * q, 8), lanes] - base
            key = ((row & (WORDS - 1)) * FIELDS) | (row >> 8)
            fits = ((row >> 11) == 0) & (slot + 8 * q < used)
            keys[q, pl.ds(pl.multiple_of(t * 8, 8), 8), :] = jnp.where(fits, key, -1)
        return carry

    lax.fori_loop(0, SAMPLES // 128, block, 0)


def compact(keys, words, adds, spill):
    spill[...] = jnp.full((8, 128), -1, jnp.int32)

    def block(b, carry):
        kept = [jnp.full((8, 128), -1, jnp.int32)] * KEPT
        lost = spill[...]
        for k in range(SLOTS):
            new = keys[k // 8, pl.ds(b * 64 + k % 8, 8, stride=8), :]
            for j in range(min(k + 1, KEPT)):
                kept[j], new = jnp.maximum(kept[j], new), jnp.minimum(kept[j], new)
            if k >= KEPT:
                lost = jnp.maximum(lost, new)
        spill[...] = lost
        word = [key >> 3 for key in kept]
        add = [jnp.where(key < 0, 0, jnp.left_shift(jnp.int32(1), (key & 7) * 4)) for key in kept]
        for j in range(KEPT - 1):
            same = word[j] == word[j + 1]
            add[j + 1] = add[j + 1] + jnp.where(same, add[j], 0)
            word[j] = jnp.where(same, -1, word[j])
        place = pl.ds(pl.multiple_of(b * 8, 8), 8)
        for j in range(KEPT):
            words[j, place, :] = word[j]
            adds[j, place, :] = add[j]
        return carry

    lax.fori_loop(0, SAMPLES // 1024, block, 0)


def count(words, adds, counts, slot):
    rows = lax.broadcasted_iota(jnp.int32, (16, 128), 0)
    for half in range(2):
        t = slot * 2 + half
        word = [jnp.broadcast_to(words[j, pl.ds(t, 1), :], (16, 128)) for j in range(KEPT)]
        add = [jnp.broadcast_to(adds[j, pl.ds(t, 1), :], (16, 128)) for j in range(KEPT)]

        def block(i, carry):
            here = rows + i * 16
            total = jnp.zeros((16, 128), jnp.int32)
            for j in range(KEPT):
                total = jnp.where(word[j] == here, add[j], total)
            for f in range(FIELDS):
                if f < FIELDS - 1:
                    part = total & (15 << (4 * f))
                else:
                    part = lax.shift_right_logical(total, 28)
                at = pl.multiple_of(f * WORDS + i * 16, 16)
                counts[slot, pl.ds(at, 16), pl.ds(half * 128, 128)] = part.astype(jnp.float32).astype(jnp.bfloat16)
            return carry

        lax.fori_loop(0, WORDS // 16, block, 0, unroll=4)


def multiply(counts, everything, total, slots, rows=slice(None)):
    part = total[rows, :]
    for slot in slots:
        part = part + jnp.dot(counts[slot, rows, :], everything[slot], preferred_element_type=jnp.float32)
    total[rows, :] = part


def towards(group, first, last, do):
    x, z = group // DEPTH, group % DEPTH
    span = last - first

    def step(i, carry):
        there = first + lax.rem(z + i, span)
        for dx in (2, 1, 3, 0):
            device = lax.rem(x + dx, WIDTH) * DEPTH + there

            @pl.when(device != group)
            def _():
                do(device)

        return carry

    lax.fori_loop(0, span, step, 0)


def greet(barrier, group, row, near, early):
    def signal(group_there, row_there):
        pl.semaphore_signal(barrier, inc=1, device_id=(group_there, row_there), device_id_type=MESH)

    @pl.when(early)
    def _():
        towards(group, EARLY, DEPTH, lambda device: signal(device, row))
        towards(group, 0, EARLY, lambda device: signal(device, row))

    for peer in near:
        signal(group, peer)


def swap(group, row, early, outgoing, incoming, swap_send, swap_recv, late_sem, all_sem, meanwhile):
    x, z = group // DEPTH, group % DEPTH

    def send(target):
        pltpu.make_async_remote_copy(
            src_ref=outgoing.at[target], dst_ref=incoming.at[group], send_sem=swap_send, recv_sem=swap_recv,
            device_id=(target, row), device_id_type=MESH,
        ).start()

    def tell(semaphore, target):
        pl.semaphore_signal(semaphore, inc=1, device_id=(target, row), device_id_type=MESH)

    towards(group, 0, EARLY, send)

    @pl.when(jnp.logical_not(early))
    def _():
        towards(group, 0, EARLY, lambda target: tell(late_sem, target))

    meanwhile()

    @pl.when(early)
    def _():
        pl.semaphore_wait(late_sem, WIDTH * (DEPTH - EARLY))
        for partner in range(EARLY, DEPTH, EARLY):

            @pl.when(z + partner < DEPTH)
            def _():
                tell(all_sem, x * DEPTH + z + partner)

    @pl.when(jnp.logical_not(early))
    def _():
        pl.semaphore_wait(all_sem, 1)

    towards(group, EARLY, DEPTH, send)


def exchange_kernel(
    grads_hbm, ids_hbm, lens_hbm, sums_hbm, gathered_hbm, spill_hbm,
    grads, ids, lens, outgoing, incoming, everything, keys, words, adds, counts, total, spill,
    load_sem, sum_sem, out_sem, swap_send, swap_recv, late_sem, all_sem, ring_send, ring_recv,
):
    group = lax.axis_index("group")
    row = lax.axis_index("row")
    z = group % DEPTH
    y, core = row // 2, row % 2

    def at(step, other):
        return lax.rem(y + step + RINGS, RINGS) * 2 + (1 - core if other else core)

    loads = [
        pltpu.make_async_copy(grads_hbm, grads, load_sem.at[0]),
        pltpu.make_async_copy(ids_hbm, ids, load_sem.at[1]),
        pltpu.make_async_copy(lens_hbm, lens, load_sem.at[2]),
    ]
    for load in loads:
        load.start()

    barrier = pltpu.get_barrier_semaphore()
    near = [at(2, False), at(-2, False), at(1, False), at(-1, False), at(0, True)]
    early = z < EARLY
    greet(barrier, group, row, near, early)
    loads[0].wait()
    outgoing[...] = jnp.swapaxes(grads[...].astype(jnp.float32), 0, 1).astype(jnp.bfloat16)
    incoming[group] = outgoing[group]

    def count_all():
        loads[1].wait()
        loads[2].wait()
        prepare(ids, lens, keys, row * TOUCHED)
        compact(keys, words, adds, spill)

        def one(slot, carry):
            count(words, adds, counts, slot)
            return carry

        lax.fori_loop(0, SHARDS, one, 0)
        total[...] = jnp.zeros((TOUCHED, E), jnp.float32)

    pl.semaphore_wait(barrier, jnp.where(early, WIDTH * EARLY - 1, WIDTH * EARLY) + len(near))
    swap(group, row, early, outgoing, incoming, swap_send, swap_recv, late_sem, all_sem, count_all)

    swapped = pltpu.make_async_copy(incoming.at[pl.ds(0, GROUPS - 1)], incoming.at[pl.ds(0, GROUPS - 1)], swap_recv)
    swapped.wait()
    everything[row] = incoming[...].astype(jnp.float32).reshape(CHUNK, E).astype(jnp.bfloat16)

    sent = []
    kept = []

    def pass_on(slot, peer):
        copy = pltpu.make_async_remote_copy(
            src_ref=everything.at[slot], dst_ref=everything.at[slot], send_sem=ring_send.at[len(sent)],
            recv_sem=ring_recv.at[slot], device_id=(group, peer), device_id_type=MESH,
        )
        copy.start()
        sent.append(copy)

    def keep(slot):
        copy = pltpu.make_async_copy(everything.at[slot], gathered_hbm.at[slot], out_sem.at[len(kept)])
        copy.start()
        kept.append(copy)

    def arrive(slot):
        pltpu.make_async_copy(everything.at[slot], everything.at[slot], ring_recv.at[slot]).wait()

    mine = [at(s, False) for s in range(RINGS)]
    theirs = [at(s, True) for s in range(RINGS)]
    for peer in near:
        pass_on(row, peer)
    keep(row)
    arrive(theirs[0])
    keep(theirs[0])
    multiply(counts, everything, total, [row, theirs[0]])
    for s in (-2, 2):
        arrive(mine[s])
    way = 1 - 2 * core
    pass_on(at(-2 * way, False), at(2 * way, False))
    pass_on(mine[-2], mine[1])
    pass_on(mine[2], mine[-1])
    pass_on(mine[-2], theirs[0])
    pass_on(mine[2], theirs[0])
    for s in (-1, 1):
        arrive(mine[s])
        pass_on(mine[s], theirs[0])
    multiply(counts, everything, total, [mine[s] for s in (-2, 2, -1, 1)])
    for s in (-2, 2, -1, 1):
        arrive(theirs[s])
    multiply(counts, everything, total, [theirs[s] for s in (-2, 2, -1, 1)])
    for s in (-2, 2, -1, 1):
        keep(mine[s])
        keep(theirs[s])
    for s in (-3, 3, 4):
        arrive(mine[s])
        pass_on(mine[s], theirs[0])
    multiply(counts, everything, total, [mine[s] for s in (-3, 3, 4)])
    for s in (-3, 3, 4):
        keep(mine[s])
    for s in (-3, 3, 4):
        arrive(theirs[s])
        keep(theirs[s])
    written = [pltpu.make_async_copy(spill, spill_hbm, load_sem.at[3])]
    written[0].start()
    for i in range(BLOCKS):
        at_rows = pl.ds(i * BLOCK, BLOCK)
        multiply(counts, everything, total, [theirs[s] for s in (-3, 3, 4)], at_rows)
        written.append(pltpu.make_async_copy(total.at[at_rows], sums_hbm.at[at_rows], sum_sem.at[i]))
        written[-1].start()
    pltpu.make_async_copy(outgoing.at[pl.ds(0, GROUPS - 1)], outgoing.at[pl.ds(0, GROUPS - 1)], swap_send).wait()
    for copy in sent:
        copy.wait_send()
    for copy in kept + written:
        copy.wait()


def update_kernel(
    sums_hbm, spill_hbm, rows_hbm, state_hbm, ids_hbm, lens_hbm, gathered_hbm, new_rows_hbm, new_state_hbm,
    sums, spill, rows, state, new_rows, new_state, ids, lens, grads, sum_sem, row_sem, out_sem, sem,
):
    parts = [pl.ds(i * PART, PART) for i in range(PARTS)]
    spill_load = pltpu.make_async_copy(spill_hbm, spill, sem.at[0])
    state_load = pltpu.make_async_copy(state_hbm, state, sem.at[1])
    sum_loads = [pltpu.make_async_copy(sums_hbm.at[at], sums.at[at], sum_sem.at[i]) for i, at in enumerate(parts)]
    row_loads = [pltpu.make_async_copy(rows_hbm.at[at], rows.at[at], row_sem.at[i]) for i, at in enumerate(parts)]
    state_load.start()
    for sum_load, row_load in zip(sum_loads, row_loads):
        sum_load.start()
        row_load.start()
    spill_load.start()

    def finish(first):
        outs = []
        for i, at_part in enumerate(parts):
            if first:
                sum_loads[i].wait()
                row_loads[i].wait()
            for j in range(i * PART // 128, (i + 1) * PART // 128):
                at = pl.ds(j * 128, 128)
                part = sums[at, :]
                if first:
                    field = j * 128 // WORDS
                    part = part * (2.0 ** (-4 * field) if field < FIELDS - 1 else 1.0)
                fresh = state[:, at] + jnp.sum((part * part).T, axis=0, keepdims=True) * (1.0 / E)
                new_state[:, at] = fresh
                scale = 0.5 / (jnp.sqrt(fresh) + 1e-08)
                new_rows[at, :] = rows[at, :] - part * jnp.broadcast_to(scale, (128, 128)).T
            outs.append(pltpu.make_async_copy(new_rows.at[at_part], new_rows_hbm.at[at_part], out_sem.at[i]))
            outs[-1].start()
        outs.append(pltpu.make_async_copy(new_state, new_state_hbm, out_sem.at[PARTS]))
        outs[-1].start()
        return outs

    state_load.wait()
    outs = finish(True)
    spill_load.wait()
    spilled = jnp.max(spill[...]) >= 0
    for out in outs:
        out.wait()

    @pl.when(spilled)
    def _():
        base = lax.axis_index("row") * TOUCHED
        for source, target in ((ids_hbm, ids), (lens_hbm, lens), (gathered_hbm, grads)):
            copy = pltpu.make_async_copy(source, target, sem.at[2])
            copy.start()
            copy.wait()
        exact = sums
        exact[...] = jnp.zeros((TOUCHED, E), jnp.float32)
        column = lax.broadcasted_iota(jnp.int32, (128, 128), 0)

        def samples(t, carry):
            lanes = pl.ds(pl.multiple_of(t * 128, 128), 128)
            part = grads[t // 2, pl.ds(pl.multiple_of((t % 2) * 128, 128), 128), :]
            used = lens[:, lanes]

            def touched(i, carry):
                here = column + (base + i * 128)

                def add(q, found):
                    eight = ids[pl.ds(pl.multiple_of(q * 8, 8), 8), lanes]
                    for s in range(8):
                        hit = (eight[s : s + 1] == here) & (q * 8 + s < used)
                        found = found + jnp.where(hit, 1.0, 0.0)
                    return found

                found = lax.fori_loop(0, SLOTS // 8, add, jnp.zeros((128, 128), jnp.float32))
                at = pl.ds(pl.multiple_of(i * 128, 128), 128)
                exact[at, :] = exact[at, :] + jnp.dot(
                    found.astype(jnp.bfloat16), part, preferred_element_type=jnp.float32
                )
                return carry

            return lax.fori_loop(0, TOUCHED // 128, touched, carry)

        lax.fori_loop(0, SAMPLES // 128, samples, 0)
        for out in finish(False):
            out.wait()


def on_device(pooled_grad, bag_ids, bag_len, table_rows, row_state):
    ids = bag_ids.reshape(SLOTS, SAMPLES)
    rows = table_rows.reshape(TOUCHED, E)
    hbm = pl.BlockSpec(memory_space=pltpu.HBM)
    sums, gathered, spill = pl.pallas_call(
        exchange_kernel,
        out_shape=(
            jax.ShapeDtypeStruct((TOUCHED, E), jnp.float32),
            jax.ShapeDtypeStruct((SHARDS, CHUNK, E), jnp.bfloat16),
            jax.ShapeDtypeStruct((8, 128), jnp.int32),
        ),
        in_specs=[hbm] * 3,
        out_specs=(hbm,) * 3,
        scratch_shapes=[
            pltpu.VMEM((SAMPLES // SHARDS // GROUPS, GROUPS, E), jnp.bfloat16),
            pltpu.VMEM((SLOTS, SAMPLES), jnp.int32),
            pltpu.VMEM((1, SAMPLES), jnp.int32),
            pltpu.VMEM((GROUPS, CHUNK // GROUPS, E), jnp.bfloat16),
            pltpu.VMEM((GROUPS, CHUNK // GROUPS, E), jnp.bfloat16),
            pltpu.VMEM((SHARDS, CHUNK, E), jnp.bfloat16),
            pltpu.VMEM((SLOTS // 8, SAMPLES // 16, 128), jnp.int32),
            pltpu.VMEM((KEPT, SAMPLES // 128, 128), jnp.int32),
            pltpu.VMEM((KEPT, SAMPLES // 128, 128), jnp.int32),
            pltpu.VMEM((SHARDS, TOUCHED, CHUNK), jnp.bfloat16),
            pltpu.VMEM((TOUCHED, E), jnp.float32),
            pltpu.VMEM((8, 128), jnp.int32),
            pltpu.SemaphoreType.DMA((4,)),
            pltpu.SemaphoreType.DMA((BLOCKS,)),
            pltpu.SemaphoreType.DMA((SHARDS,)),
            pltpu.SemaphoreType.DMA,
            pltpu.SemaphoreType.DMA,
            pltpu.SemaphoreType.REGULAR,
            pltpu.SemaphoreType.REGULAR,
            pltpu.SemaphoreType.DMA((16,)),
            pltpu.SemaphoreType.DMA((SHARDS,)),
        ],
        compiler_params=pltpu.CompilerParams(collective_id=0, has_side_effects=True, vmem_limit_bytes=VMEM),
        name="exchange_and_count",
    )(pooled_grad, ids, bag_len)
    new_rows, new_state = pl.pallas_call(
        update_kernel,
        out_shape=(
            jax.ShapeDtypeStruct((TOUCHED, E), jnp.float32),
            jax.ShapeDtypeStruct((1, TOUCHED), jnp.float32),
        ),
        in_specs=[hbm] * 7,
        out_specs=(hbm, hbm),
        scratch_shapes=[
            pltpu.VMEM((TOUCHED, E), jnp.float32),
            pltpu.VMEM((8, 128), jnp.int32),
            pltpu.VMEM((TOUCHED, E), jnp.float32),
            pltpu.VMEM((1, TOUCHED), jnp.float32),
            pltpu.VMEM((TOUCHED, E), jnp.float32),
            pltpu.VMEM((1, TOUCHED), jnp.float32),
            pltpu.VMEM((SLOTS, SAMPLES), jnp.int32),
            pltpu.VMEM((1, SAMPLES), jnp.int32),
            pltpu.VMEM((SHARDS, CHUNK, E), jnp.bfloat16),
            pltpu.SemaphoreType.DMA((PARTS,)),
            pltpu.SemaphoreType.DMA((PARTS,)),
            pltpu.SemaphoreType.DMA((PARTS + 1,)),
            pltpu.SemaphoreType.DMA((3,)),
        ],
        compiler_params=pltpu.CompilerParams(vmem_limit_bytes=VMEM),
        name="update",
    )(sums, spill, rows, row_state, ids, bag_len, gathered)
    return (new_rows.reshape(1, TOUCHED, E), new_state)


def solution(mesh):
    placed = (
        P(("row", "group"), None, None),
        P("group", None, None),
        P("group", None),
        P("group", "row", None),
        P("group", "row"),
    )
    return jax.shard_map(
        on_device,
        mesh=mesh,
        in_specs=placed,
        out_specs=(P("group", "row", None), P("group", "row")),
        check_vma=False,
    )
```

```python
import functools

import jax
import jax.numpy as jnp
from jax import lax
from jax.experimental import pallas as pl
from jax.experimental.pallas import tpu as pltpu
from jax.sharding import PartitionSpec as P

E = 128
SLOTS = 40
SAMPLES = 4096
GROUPS = 64
SHARDS = 16
WIDTH = 4
DEPTH = 16
RINGS = 8
EARLY = 7
VMEM = 60 * 2**20
TOUCHED = 2048
BLOCKS = 4
BLOCK = TOUCHED // BLOCKS
PARTS = 4
PART = TOUCHED // PARTS
FIELDS = 8
WORDS = TOUCHED // FIELDS
KEPT = 15
CHUNK = SAMPLES // SHARDS
MESH = pl.DeviceIdType.MESH


def prepare(ids, lens, keys, base):
    slot = lax.broadcasted_iota(jnp.int32, (8, 128), 0)

    def block(t, carry):
        lanes = pl.ds(pl.multiple_of(t * 128, 128), 128)
        used = lens[:, lanes]
        for q in range(SLOTS // 8):
            row = ids[pl.ds(8 * q, 8), lanes] - base
            key = ((row & (WORDS - 1)) * FIELDS) | (row >> 8)
            fits = ((row >> 11) == 0) & (slot + 8 * q < used)
            keys[q, pl.ds(pl.multiple_of(t * 8, 8), 8), :] = jnp.where(fits, key, -1)
        return carry

    lax.fori_loop(0, SAMPLES // 128, block, 0)


def compact(keys, words, adds, spill):
    spill[...] = jnp.full((8, 128), -1, jnp.int32)

    def block(b, carry):
        kept = [jnp.full((8, 128), -1, jnp.int32)] * KEPT
        lost = spill[...]
        for k in range(SLOTS):
            new = keys[k // 8, pl.ds(b * 64 + k % 8, 8, stride=8), :]
            for j in range(min(k + 1, KEPT)):
                kept[j], new = jnp.maximum(kept[j], new), jnp.minimum(kept[j], new)
            if k >= KEPT:
                lost = jnp.maximum(lost, new)
        spill[...] = lost
        word = [key >> 3 for key in kept]
        add = [jnp.where(key < 0, 0, jnp.left_shift(jnp.int32(1), (key & 7) * 4)) for key in kept]
        for j in range(KEPT - 1):
            same = word[j] == word[j + 1]
            add[j + 1] = add[j + 1] + jnp.where(same, add[j], 0)
            word[j] = jnp.where(same, -1, word[j])
        place = pl.ds(pl.multiple_of(b * 8, 8), 8)
        for j in range(KEPT):
            words[j, place, :] = word[j]
            adds[j, place, :] = add[j]
        return carry

    lax.fori_loop(0, SAMPLES // 1024, block, 0)


def count(words, adds, counts, slot):
    rows = lax.broadcasted_iota(jnp.int32, (16, 128), 0)
    for half in range(2):
        t = slot * 2 + half
        word = [jnp.broadcast_to(words[j, pl.ds(t, 1), :], (16, 128)) for j in range(KEPT)]
        add = [jnp.broadcast_to(adds[j, pl.ds(t, 1), :], (16, 128)) for j in range(KEPT)]

        def block(i, carry):
            here = rows + i * 16
            total = jnp.zeros((16, 128), jnp.int32)
            for j in range(KEPT):
                total = jnp.where(word[j] == here, add[j], total)
            for f in range(FIELDS):
                if f < FIELDS - 1:
                    part = total & (15 << (4 * f))
                else:
                    part = lax.shift_right_logical(total, 28)
                at = pl.multiple_of(f * WORDS + i * 16, 16)
                counts[slot, pl.ds(at, 16), pl.ds(half * 128, 128)] = part.astype(jnp.float32).astype(jnp.bfloat16)
            return carry

        lax.fori_loop(0, WORDS // 16, block, 0, unroll=4)


def multiply(counts, everything, total, slots, rows=slice(None)):
    part = total[rows, :]
    for slot in slots:
        part = part + jnp.dot(counts[slot, rows, :], everything[slot], preferred_element_type=jnp.float32)
    total[rows, :] = part


def towards(group, first, last, do):
    x, z = group // DEPTH, group % DEPTH
    span = last - first

    def step(i, carry):
        there = first + lax.rem(z + i, span)
        for dx in (2, 1, 3, 0):
            device = lax.rem(x + dx, WIDTH) * DEPTH + there

            @pl.when(device != group)
            def _():
                do(device)

        return carry

    lax.fori_loop(0, span, step, 0)


def greet(barrier, group, row, near, early):
    def signal(group_there, row_there):
        pl.semaphore_signal(barrier, inc=1, device_id=(group_there, row_there), device_id_type=MESH)

    @pl.when(early)
    def _():
        towards(group, EARLY, DEPTH, lambda device: signal(device, row))
        towards(group, 0, EARLY, lambda device: signal(device, row))

    for peer in near:
        signal(group, peer)


def swap(group, row, early, outgoing, incoming, swap_send, swap_recv, late_sem, all_sem, meanwhile):
    x, z = group // DEPTH, group % DEPTH

    def send(target):
        pltpu.make_async_remote_copy(
            src_ref=outgoing.at[target], dst_ref=incoming.at[group], send_sem=swap_send, recv_sem=swap_recv,
            device_id=(target, row), device_id_type=MESH,
        ).start()

    def tell(semaphore, target):
        pl.semaphore_signal(semaphore, inc=1, device_id=(target, row), device_id_type=MESH)

    towards(group, 0, EARLY, send)

    @pl.when(jnp.logical_not(early))
    def _():
        towards(group, 0, EARLY, lambda target: tell(late_sem, target))

    meanwhile()

    @pl.when(early)
    def _():
        pl.semaphore_wait(late_sem, WIDTH * (DEPTH - EARLY))
        for there in range(EARLY, DEPTH):
            source = EARLY - 1 if there - (EARLY - 1) <= DEPTH - there else 0

            @pl.when(z == source)
            def _(there=there):
                tell(all_sem, x * DEPTH + there)

    @pl.when(jnp.logical_not(early))
    def _():
        pl.semaphore_wait(all_sem, 1)

    towards(group, EARLY, DEPTH, send)


def exchange_kernel(
    grads_hbm, ids_hbm, lens_hbm, sums_hbm, gathered_hbm, spill_hbm,
    grads, ids, lens, outgoing, incoming, everything, keys, words, adds, counts, total, spill,
    load_sem, sum_sem, out_sem, swap_send, swap_recv, late_sem, all_sem, ring_send, ring_recv,
):
    group = lax.axis_index("group")
    row = lax.axis_index("row")
    z = group % DEPTH
    y, core = row // 2, row % 2

    def at(step, other):
        return lax.rem(y + step + RINGS, RINGS) * 2 + (1 - core if other else core)

    loads = [
        pltpu.make_async_copy(grads_hbm, grads, load_sem.at[0]),
        pltpu.make_async_copy(ids_hbm, ids, load_sem.at[1]),
        pltpu.make_async_copy(lens_hbm, lens, load_sem.at[2]),
    ]
    for load in loads:
        load.start()

    barrier = pltpu.get_barrier_semaphore()
    near = [at(2, False), at(-2, False), at(1, False), at(-1, False), at(0, True)]
    early = z < EARLY
    greet(barrier, group, row, near, early)
    loads[0].wait()
    outgoing[...] = jnp.swapaxes(grads[...].astype(jnp.float32), 0, 1).astype(jnp.bfloat16)
    incoming[group] = outgoing[group]

    def count_all():
        loads[1].wait()
        loads[2].wait()
        prepare(ids, lens, keys, row * TOUCHED)
        compact(keys, words, adds, spill)

        def one(slot, carry):
            count(words, adds, counts, slot)
            return carry

        lax.fori_loop(0, SHARDS, one, 0)
        total[...] = jnp.zeros((TOUCHED, E), jnp.float32)

    pl.semaphore_wait(barrier, jnp.where(early, WIDTH * EARLY - 1, WIDTH * EARLY) + len(near))
    swap(group, row, early, outgoing, incoming, swap_send, swap_recv, late_sem, all_sem, count_all)

    swapped = pltpu.make_async_copy(incoming.at[pl.ds(0, GROUPS - 1)], incoming.at[pl.ds(0, GROUPS - 1)], swap_recv)
    swapped.wait()
    everything[row] = incoming[...].astype(jnp.float32).reshape(CHUNK, E).astype(jnp.bfloat16)

    sent = []
    kept = []

    def pass_on(slot, peer):
        copy = pltpu.make_async_remote_copy(
            src_ref=everything.at[slot], dst_ref=everything.at[slot], send_sem=ring_send.at[len(sent)],
            recv_sem=ring_recv.at[slot], device_id=(group, peer), device_id_type=MESH,
        )
        copy.start()
        sent.append(copy)

    def keep(slot):
        copy = pltpu.make_async_copy(everything.at[slot], gathered_hbm.at[slot], out_sem.at[len(kept)])
        copy.start()
        kept.append(copy)

    def arrive(slot):
        pltpu.make_async_copy(everything.at[slot], everything.at[slot], ring_recv.at[slot]).wait()

    mine = [at(s, False) for s in range(RINGS)]
    theirs = [at(s, True) for s in range(RINGS)]
    for peer in near:
        pass_on(row, peer)
    keep(row)
    arrive(theirs[0])
    keep(theirs[0])
    multiply(counts, everything, total, [row, theirs[0]])
    for s in (-2, 2):
        arrive(mine[s])
    way = 1 - 2 * core
    pass_on(at(-2 * way, False), at(2 * way, False))
    pass_on(mine[-2], mine[1])
    pass_on(mine[2], mine[-1])
    pass_on(mine[-2], theirs[0])
    pass_on(mine[2], theirs[0])
    for s in (-1, 1):
        arrive(mine[s])
        pass_on(mine[s], theirs[0])
    multiply(counts, everything, total, [mine[s] for s in (-2, 2, -1, 1)])
    for s in (-2, 2, -1, 1):
        arrive(theirs[s])
    multiply(counts, everything, total, [theirs[s] for s in (-2, 2, -1, 1)])
    for s in (-2, 2, -1, 1):
        keep(mine[s])
        keep(theirs[s])
    for s in (-3, 3, 4):
        arrive(mine[s])
        pass_on(mine[s], theirs[0])
    multiply(counts, everything, total, [mine[s] for s in (-3, 3, 4)])
    for s in (-3, 3, 4):
        keep(mine[s])
    for s in (-3, 3, 4):
        arrive(theirs[s])
        keep(theirs[s])
    written = [pltpu.make_async_copy(spill, spill_hbm, load_sem.at[3])]
    written[0].start()
    for i in range(BLOCKS):
        at_rows = pl.ds(i * BLOCK, BLOCK)
        multiply(counts, everything, total, [theirs[s] for s in (-3, 3, 4)], at_rows)
        written.append(pltpu.make_async_copy(total.at[at_rows], sums_hbm.at[at_rows], sum_sem.at[i]))
        written[-1].start()
    pltpu.make_async_copy(outgoing.at[pl.ds(0, GROUPS - 1)], outgoing.at[pl.ds(0, GROUPS - 1)], swap_send).wait()
    for copy in sent:
        copy.wait_send()
    for copy in kept + written:
        copy.wait()


def update_kernel(
    sums_hbm, spill_hbm, rows_hbm, state_hbm, ids_hbm, lens_hbm, gathered_hbm, new_rows_hbm, new_state_hbm,
    sums, spill, rows, state, new_rows, new_state, ids, lens, grads, sum_sem, row_sem, out_sem, sem,
):
    parts = [pl.ds(i * PART, PART) for i in range(PARTS)]
    spill_load = pltpu.make_async_copy(spill_hbm, spill, sem.at[0])
    state_load = pltpu.make_async_copy(state_hbm, state, sem.at[1])
    sum_loads = [pltpu.make_async_copy(sums_hbm.at[at], sums.at[at], sum_sem.at[i]) for i, at in enumerate(parts)]
    row_loads = [pltpu.make_async_copy(rows_hbm.at[at], rows.at[at], row_sem.at[i]) for i, at in enumerate(parts)]
    state_load.start()
    for sum_load, row_load in zip(sum_loads, row_loads):
        sum_load.start()
        row_load.start()
    spill_load.start()

    def finish(first):
        outs = []
        for i, at_part in enumerate(parts):
            if first:
                sum_loads[i].wait()
                row_loads[i].wait()
            for j in range(i * PART // 128, (i + 1) * PART // 128):
                at = pl.ds(j * 128, 128)
                part = sums[at, :]
                if first:
                    field = j * 128 // WORDS
                    part = part * (2.0 ** (-4 * field) if field < FIELDS - 1 else 1.0)
                fresh = state[:, at] + jnp.sum((part * part).T, axis=0, keepdims=True) * (1.0 / E)
                new_state[:, at] = fresh
                scale = 0.5 / (jnp.sqrt(fresh) + 1e-08)
                new_rows[at, :] = rows[at, :] - part * jnp.broadcast_to(scale, (128, 128)).T
            outs.append(pltpu.make_async_copy(new_rows.at[at_part], new_rows_hbm.at[at_part], out_sem.at[i]))
            outs[-1].start()
        outs.append(pltpu.make_async_copy(new_state, new_state_hbm, out_sem.at[PARTS]))
        outs[-1].start()
        return outs

    state_load.wait()
    outs = finish(True)
    spill_load.wait()
    spilled = jnp.max(spill[...]) >= 0
    for out in outs:
        out.wait()

    @pl.when(spilled)
    def _():
        base = lax.axis_index("row") * TOUCHED
        for source, target in ((ids_hbm, ids), (lens_hbm, lens), (gathered_hbm, grads)):
            copy = pltpu.make_async_copy(source, target, sem.at[2])
            copy.start()
            copy.wait()
        exact = sums
        exact[...] = jnp.zeros((TOUCHED, E), jnp.float32)
        column = lax.broadcasted_iota(jnp.int32, (128, 128), 0)

        def samples(t, carry):
            lanes = pl.ds(pl.multiple_of(t * 128, 128), 128)
            part = grads[t // 2, pl.ds(pl.multiple_of((t % 2) * 128, 128), 128), :]
            used = lens[:, lanes]

            def touched(i, carry):
                here = column + (base + i * 128)

                def add(q, found):
                    eight = ids[pl.ds(pl.multiple_of(q * 8, 8), 8), lanes]
                    for s in range(8):
                        hit = (eight[s : s + 1] == here) & (q * 8 + s < used)
                        found = found + jnp.where(hit, 1.0, 0.0)
                    return found

                found = lax.fori_loop(0, SLOTS // 8, add, jnp.zeros((128, 128), jnp.float32))
                at = pl.ds(pl.multiple_of(i * 128, 128), 128)
                exact[at, :] = exact[at, :] + jnp.dot(
                    found.astype(jnp.bfloat16), part, preferred_element_type=jnp.float32
                )
                return carry

            return lax.fori_loop(0, TOUCHED // 128, touched, carry)

        lax.fori_loop(0, SAMPLES // 128, samples, 0)
        for out in finish(False):
            out.wait()


def on_device(pooled_grad, bag_ids, bag_len, table_rows, row_state):
    ids = bag_ids.reshape(SLOTS, SAMPLES)
    rows = table_rows.reshape(TOUCHED, E)
    hbm = pl.BlockSpec(memory_space=pltpu.HBM)
    sums, gathered, spill = pl.pallas_call(
        exchange_kernel,
        out_shape=(
            jax.ShapeDtypeStruct((TOUCHED, E), jnp.float32),
            jax.ShapeDtypeStruct((SHARDS, CHUNK, E), jnp.bfloat16),
            jax.ShapeDtypeStruct((8, 128), jnp.int32),
        ),
        in_specs=[hbm] * 3,
        out_specs=(hbm,) * 3,
        scratch_shapes=[
            pltpu.VMEM((SAMPLES // SHARDS // GROUPS, GROUPS, E), jnp.bfloat16),
            pltpu.VMEM((SLOTS, SAMPLES), jnp.int32),
            pltpu.VMEM((1, SAMPLES), jnp.int32),
            pltpu.VMEM((GROUPS, CHUNK // GROUPS, E), jnp.bfloat16),
            pltpu.VMEM((GROUPS, CHUNK // GROUPS, E), jnp.bfloat16),
            pltpu.VMEM((SHARDS, CHUNK, E), jnp.bfloat16),
            pltpu.VMEM((SLOTS // 8, SAMPLES // 16, 128), jnp.int32),
            pltpu.VMEM((KEPT, SAMPLES // 128, 128), jnp.int32),
            pltpu.VMEM((KEPT, SAMPLES // 128, 128), jnp.int32),
            pltpu.VMEM((SHARDS, TOUCHED, CHUNK), jnp.bfloat16),
            pltpu.VMEM((TOUCHED, E), jnp.float32),
            pltpu.VMEM((8, 128), jnp.int32),
            pltpu.SemaphoreType.DMA((4,)),
            pltpu.SemaphoreType.DMA((BLOCKS,)),
            pltpu.SemaphoreType.DMA((SHARDS,)),
            pltpu.SemaphoreType.DMA,
            pltpu.SemaphoreType.DMA,
            pltpu.SemaphoreType.REGULAR,
            pltpu.SemaphoreType.REGULAR,
            pltpu.SemaphoreType.DMA((16,)),
            pltpu.SemaphoreType.DMA((SHARDS,)),
        ],
        compiler_params=pltpu.CompilerParams(collective_id=0, has_side_effects=True, vmem_limit_bytes=VMEM),
        name="exchange_and_count",
    )(pooled_grad, ids, bag_len)
    new_rows, new_state = pl.pallas_call(
        update_kernel,
        out_shape=(
            jax.ShapeDtypeStruct((TOUCHED, E), jnp.float32),
            jax.ShapeDtypeStruct((1, TOUCHED), jnp.float32),
        ),
        in_specs=[hbm] * 7,
        out_specs=(hbm, hbm),
        scratch_shapes=[
            pltpu.VMEM((TOUCHED, E), jnp.float32),
            pltpu.VMEM((8, 128), jnp.int32),
            pltpu.VMEM((TOUCHED, E), jnp.float32),
            pltpu.VMEM((1, TOUCHED), jnp.float32),
            pltpu.VMEM((TOUCHED, E), jnp.float32),
            pltpu.VMEM((1, TOUCHED), jnp.float32),
            pltpu.VMEM((SLOTS, SAMPLES), jnp.int32),
            pltpu.VMEM((1, SAMPLES), jnp.int32),
            pltpu.VMEM((SHARDS, CHUNK, E), jnp.bfloat16),
            pltpu.SemaphoreType.DMA((PARTS,)),
            pltpu.SemaphoreType.DMA((PARTS,)),
            pltpu.SemaphoreType.DMA((PARTS + 1,)),
            pltpu.SemaphoreType.DMA((3,)),
        ],
        compiler_params=pltpu.CompilerParams(vmem_limit_bytes=VMEM),
        name="update",
    )(sums, spill, rows, row_state, ids, bag_len, gathered)
    return (new_rows.reshape(1, TOUCHED, E), new_state)


def solution(mesh):
    placed = (
        P(("row", "group"), None, None),
        P("group", None, None),
        P("group", None),
        P("group", "row", None),
        P("group", "row"),
    )
    return jax.shard_map(
        on_device,
        mesh=mesh,
        in_specs=placed,
        out_specs=(P("group", "row", None), P("group", "row")),
        check_vma=False,
    )
```
